128 devices in a mesh: outer: 16 (over x_hi, y, core), inner: 8 (over z, x_lo).
Axes of the slice: x: 4 (x_hi: 2, x_lo: 2; x = x_hi * 2 + x_lo), y: 4, z: 4, core: 2. Of those that a mesh axis runs over, the one named last changes fastest.
Arguments:
- tokens: bfloat16 [65536, 8192], P(('outer', 'inner')), may hold values from -24 to 24
- key_weight: bfloat16 [8192, 512], P('inner', 'outer'), may hold values from -0.0625 to 0.0625
- cotangent: bfloat16 [65536, 512], P(('outer', 'inner')), may hold values from -6 to 6
Outputs:
- keys: bfloat16 [65536, 512], P(('outer', 'inner'))
- input_gradient: bfloat16 [65536, 8192], P(('outer', 'inner'))
- grad_weight: float32 [8192, 512], P('inner', 'outer')
The draws below stay inside these ranges and needn't reach their ends.
All inputs are finite; a program needn't handle non-finite values.
Results may differ from the reference program's by a relative error of at most 0.005.
Values may be sent and summed in bfloat16 or wider, within the bound.
No kernel may reach another device: no remote copies, remote signals or barrier semaphores. Data moves between devices by JAX's collectives and lax.ppermute only.
A program may use at most 192 MiB of HBM per device.

```python
import math
import jax
import jax.numpy as jnp
from jax import lax

D = 8192
HEAD = 128
KV_HEADS = 4
SEQ = 4096
KV_WIDTH = 512
TOKENS = 65536
N_OUTER = 16


def spiked(result, key, source, target, shards_of, factor):
    def block_of(dim):
        return (jnp.arange(result.shape[dim]) // (result.shape[dim] // shards_of)).reshape((-1,) + (1,) * (result.ndim - 1 - dim))

    one_side = jax.random.permutation(key, shards_of)[block_of(target)]
    other_side = (block_of(target) + shards_of // 2) % shards_of
    return jnp.where((block_of(source) == one_side) | (block_of(source) == other_side), factor * result, result)


def block_scale(own_key, dims, pieces, least, largest):
    gain, own = 1.0, jax.random.fold_in(own_key, 6)
    for dim, shards_of in pieces:
        draws = jnp.exp(jax.random.uniform(jax.random.fold_in(own, dim), (shards_of,), jnp.float32, least / len(pieces), largest / len(pieces)))
        gain = gain * jnp.repeat(draws, dims[dim] // shards_of).reshape([-1 if axis == dim else 1 for axis in range(len(dims))])
    return gain


def normal_values(rng, extent, scale, most, cuts=(), kind=jnp.bfloat16):
    drawn = scale * jax.random.normal(rng, extent, jnp.float32)
    if cuts:
        drawn = drawn * block_scale(rng, extent, cuts, -0.22, 0.18)
    return jnp.clip(drawn, -most, most).astype(kind)


def noise_with(rng, extent, spread, most, pieces, heavy, kind=jnp.bfloat16):
    array = spread * jax.random.normal(rng, extent, jnp.float32)
    if pieces:
        array = array * block_scale(rng, extent, pieces, -0.22, 0.18)
    return jnp.clip(spiked(array, jax.random.fold_in(rng, 3), *heavy), -most, most).astype(kind)


def setup_inputs(seed: int = 0) -> dict:
    key_of = jax.random.split(jax.random.key(seed), 4)
    tokens = noise_with(key_of[0], (TOKENS, D), 1.0, 24.0, ((0, 128),), (0, 1, 128, 5.5))
    key_weight = normal_values(key_of[1], (D, KV_WIDTH), D ** -0.5, 0.0625, ((0, 8), (1, 16)))
    cotangent = normal_values(key_of[2], (TOKENS, KV_WIDTH), 1.0, 6.0, ((0, 128),))
    return {"tokens": tokens, "key_weight": key_weight, "cotangent": cotangent}


EPS = 1e-05

def rope_tables(start, count):
    position = ((start + jnp.arange(count, dtype=jnp.int32)) % SEQ).astype(jnp.float32)
    half = HEAD // 2
    inv_freq = jnp.exp(-math.log(10000.0) * jnp.arange(half, dtype=jnp.float32) / half)
    angle = position[:, None] * inv_freq[None, :]
    return (jnp.cos(angle)[:, None, :], jnp.sin(angle)[:, None, :])

def apply_rotary(values, cosine, sine, sign):
    count = values.shape[0]
    split = values.reshape(count, KV_HEADS, 2, HEAD // 2)
    first = split[:, :, 0, :]
    second = split[:, :, 1, :]
    new_first = first * cosine - sign * second * sine
    new_second = second * cosine + sign * first * sine
    return jnp.stack([new_first, new_second], axis=2).reshape(count, KV_HEADS * HEAD)

def reference(tokens, key_weight, cotangent):
    block = TOKENS // N_OUTER

    def step(total, index):
        start = (index * block).astype(jnp.int32)
        complete_input = lax.dynamic_slice_in_dim(tokens, start, block, 0).astype(jnp.float32)
        grads = lax.dynamic_slice_in_dim(cotangent, start, block, 0).astype(jnp.float32)
        reciprocal_root_mean = lax.rsqrt(lax.optimization_barrier(jnp.mean(complete_input * complete_input, axis=1, keepdims=True)) + EPS)
        centered_input = complete_input * reciprocal_root_mean
        normalized_tokens = centered_input.astype(jnp.bfloat16)
        cosine, sine = rope_tables(start, block)
        pre = jnp.dot(normalized_tokens, key_weight, preferred_element_type=jnp.float32)
        keys = apply_rotary(pre, cosine, sine, 1.0).astype(jnp.bfloat16)
        dpre = apply_rotary(grads, cosine, sine, -1.0).astype(jnp.bfloat16)
        total = total + jnp.dot(normalized_tokens.T, dpre, preferred_element_type=jnp.float32)
        normalized_gradient = jnp.dot(dpre, key_weight.T, preferred_element_type=jnp.float32)
        input_gradient = ((normalized_gradient - centered_input * lax.optimization_barrier(jnp.mean(normalized_gradient * centered_input, axis=1, keepdims=True))) * reciprocal_root_mean).astype(jnp.bfloat16)
        return (total, (keys, input_gradient))
    total, (keys, input_gradient) = lax.scan(step, jnp.zeros((D, KV_HEADS * HEAD), jnp.float32), jnp.arange(N_OUTER, dtype=jnp.int32))
    scale = 1.0 / math.sqrt(TOKENS)
    return (keys.reshape(TOKENS, KV_HEADS * HEAD), input_gradient.reshape(TOKENS, D), total * scale)
```

```python
import math

import jax
import jax.numpy as jnp
from jax import lax
from jax.experimental import pallas as pl
from jax.experimental.pallas import tpu as pltpu
from jax.sharding import Mesh
from jax.sharding import PartitionSpec as P

HEAD = 128
KV_HEADS = 4
SEQ = 4096
EPS = 1e-05
D = 8192
KV = 512
ROWS = 512
LANES = 512
STEPS = D // (2 * LANES)
AXES = ("xh", "y", "c", "z", "xl")
MIB = 1 << 20
F32 = jnp.float32
BF16 = jnp.bfloat16


def rope_tables(start, count):
    position = ((start + jnp.arange(count, dtype=jnp.int32)) % SEQ).astype(F32)
    half = HEAD // 2
    inv_freq = jnp.exp(-math.log(10000.0) * jnp.arange(half, dtype=F32) / half)
    angle = position[:, None] * inv_freq[None, :]
    return jnp.cos(angle), jnp.sin(angle)


def both_halves(cosine, sine):
    cos, sin = cosine[...], sine[...]
    return jnp.concatenate([cos, cos], 1), jnp.concatenate([-sin, sin], 1)


def rotate(values, cosine, sine):
    return values * cosine + pltpu.roll(values, HEAD // 2, 1) * sine


def params(mib):
    return pltpu.CompilerParams(vmem_limit_bytes=mib * MIB)


SMEM = pl.BlockSpec(memory_space=pltpu.SMEM)


VMEM = pl.BlockSpec(memory_space=pltpu.VMEM)


def stay(value):
    return pltpu.with_memory_space_constraint(value, pltpu.VMEM)


def prepare_kernel(start, x, cot, cosine, sine, normed, inv, dpre, dpre_t):
    rows = pl.ds(pl.multiple_of((pl.program_id(0) + start) * 128, 128), 128)
    acc = jnp.zeros((128, 128), F32)
    for k in range(D // 128):
        wide = x[:, k * 128 : (k + 1) * 128].astype(F32)
        acc += wide * wide
    scale = lax.rsqrt(jnp.sum(acc, axis=1, keepdims=True) / D + EPS)
    scale = jnp.broadcast_to(scale, (128, 128))
    inv[rows, :] = scale
    for k in range(D // 128):
        part, col = divmod(k * 128, LANES)
        value = x[:, k * 128 : (k + 1) * 128].astype(F32) * scale
        normed[part % 2, part // 2, rows, col : col + 128] = value.astype(BF16)
    cos, sin = both_halves(cosine, sine)
    for head in range(KV_HEADS):
        cols = slice(head * HEAD, (head + 1) * HEAD)
        turned = rotate(cot[:, cols].astype(F32), cos, -sin)
        dpre[rows, cols] = turned.astype(BF16)
        dpre_t[cols, rows] = turned.T.astype(BF16)


def prepare_call(half, tokens, cot, cosine, sine, before=()):
    blocks = ROWS // 256
    rows = lambda width: pl.BlockSpec((128, width), lambda j: (j + blocks * half, 0))

    def kernel(*refs):
        prepare_kernel(half * blocks, *refs[:4], *refs[4 + len(before) :])

    return pl.pallas_call(
        kernel,
        grid=(blocks,),
        in_specs=[rows(D), rows(KV), rows(HEAD // 2), rows(HEAD // 2)] + [VMEM] * len(before),
        out_specs=[VMEM] * 4,
        out_shape=[
            pltpu.VMEM((2, STEPS, ROWS, LANES), BF16),
            pltpu.VMEM((ROWS, 128), F32),
            pltpu.VMEM((ROWS, KV), BF16),
            pltpu.VMEM((KV, ROWS), BF16),
        ],
        input_output_aliases={4 + i: i for i in range(len(before))},
        compiler_params=params(16),
        cost_estimate=pl.CostEstimate(flops=5 * ROWS * D, bytes_accessed=9 * MIB, transcendentals=0),
        name="row_scales",
    )(
        pltpu.with_memory_space_constraint(tokens, pltpu.HBM),
        pltpu.with_memory_space_constraint(cot, pltpu.HBM),
        cosine,
        sine,
        *map(stay, before),
    )


def send_kernel(core, normed, dpre_t, out):
    @pl.loop(0, STEPS)
    def _(i):
        term = jnp.dot(dpre_t[...], normed[1 - core[0], i], preferred_element_type=F32)
        out[i] = term.astype(BF16).reshape(16, 32, LANES)


def send_call(core, normed, dpre_t):
    return pl.pallas_call(
        send_kernel,
        in_specs=[SMEM, VMEM, VMEM],
        out_specs=VMEM,
        out_shape=pltpu.VMEM((STEPS, 16, 32, LANES), BF16),
        compiler_params=params(8),
        cost_estimate=pl.CostEstimate(flops=ROWS * D * KV, bytes_accessed=9 * MIB, transcendentals=0),
        name="send_half",
    )(core, stay(normed), stay(dpre_t))


def keep_kernel(core, x, y, z, normed, dpre_t, came, *rest):
    outs, total = rest[:8], rest[8]

    @pl.loop(0, STEPS)
    def _(i):
        term = jnp.dot(dpre_t[...], normed[core[0], i], preferred_element_type=F32)
        total[i] = (term.reshape(16, 32, LANES) + came[i].astype(F32)).astype(BF16)

    first = core[0] == 0
    half = LANES // 2

    @pl.loop(0, 16)
    def _(n):
        a, b = n // 4, n % 4
        for r in range(4):
            xx, yy, zz = (x[0] + r) % 4, (y[0] + r) % 4, (z[0] + r) % 4
            for h in range(2):
                x_at = jnp.where(first, xx, b)
                y_at = jnp.where(first, a, yy if h == 0 else a)
                z_at = jnp.where(first, b, a if h == 0 else zz)
                outs[4 * h + r][a, b] = total[
                    2 * z_at + x_at % 2,
                    pl.ds(8 * (x_at // 2) + 2 * y_at, 2),
                    :,
                    h * half : (h + 1) * half,
                ]


def keep_call(core, x, y, z, normed, dpre_t, came):
    part = (4, 4, 2, 32, LANES // 2)
    return pl.pallas_call(
        keep_kernel,
        in_specs=[SMEM] * 4 + [VMEM] * 3,
        out_specs=[VMEM] * 8,
        out_shape=[pltpu.VMEM(part, BF16)] * 8,
        scratch_shapes=[pltpu.VMEM((STEPS, 16, 32, LANES), BF16)],
        compiler_params=params(16),
        cost_estimate=pl.CostEstimate(flops=ROWS * D * KV, bytes_accessed=13 * MIB, transcendentals=0),
        name="keep_half",
    )(core, x, y, z, stay(normed), stay(dpre_t), stay(came))


def sum_first_kernel(core, first, second, own, one, two, three, *outs):
    base = jnp.where(core[0] == 0, first[0], second[0])
    for r in range(4):
        k = (base + r) % 4
        total = own[k].astype(F32)
        for other in (one, two, three):
            total += other[k].astype(F32)
        outs[r][...] = total.astype(BF16)


def sum_first(core, first, second, parts):
    shape = parts[0].shape
    return pl.pallas_call(
        sum_first_kernel,
        in_specs=[SMEM] * 3 + [VMEM] * 4,
        out_specs=[VMEM] * 4,
        out_shape=[pltpu.VMEM(shape[1:], BF16)] * 4,
        compiler_params=params(8),
        cost_estimate=pl.CostEstimate(flops=0, bytes_accessed=10 * math.prod(shape), transcendentals=0),
        name="sum_first",
    )(core, first, second, *map(stay, parts))


def sum_second_kernel(core, first, second, *rest):
    parts, outs = rest[:8], rest[8:]
    base = jnp.where(core[0] == 0, first[0], second[0])
    half = LANES // 2
    for r in range(4):
        k = (base + r) % 4
        for h in range(2):
            total = parts[4 * h][k].astype(F32)
            for other in parts[4 * h + 1 : 4 * h + 4]:
                total += other[k].astype(F32)
            outs[r][:, :, h * half : (h + 1) * half] = total.astype(BF16)


def sum_second(core, first, second, parts):
    return pl.pallas_call(
        sum_second_kernel,
        in_specs=[SMEM] * 3 + [VMEM] * 8,
        out_specs=[VMEM] * 4,
        out_shape=[pltpu.VMEM((2, 32, LANES), BF16)] * 4,
        compiler_params=params(8),
        cost_estimate=pl.CostEstimate(flops=0, bytes_accessed=2 * MIB, transcendentals=0),
        name="sum_second",
    )(core, first, second, *map(stay, parts))


def weight_copies(core, y, z, pieces, ws, sems):
    copies = []
    for side in range(2):
        lane = core[0] if side == 0 else 1 - core[0]
        for r in range(4):
            for k in range(4):
                down, along = jnp.where(lane == 0, r, k), jnp.where(lane == 0, k, r)
                copies.append(
                    pltpu.make_async_copy(
                        pieces[4 * side + r].at[k],
                        ws.at[lane, (z[0] + down) % 4, :, :, (y[0] + along) % 4],
                        sems.at[lane, down, along],
                    )
                )
    return copies


def keys_kernel(core, y, z, normed, dpre, cosine, sine, *rest):
    pieces, (keys, coef, ws, pre, sems) = rest[:8], rest[8:]
    for copy in weight_copies(core, y, z, pieces, ws, sems):
        copy.start()

    @pl.loop(0, 4)
    def _(n):
        down = (z[0] + n) % 4
        for lane in range(2):
            for along in range(4):
                pltpu.make_async_copy(
                    pieces[0].at[0],
                    ws.at[lane, down, :, :, (y[0] + along) % 4],
                    sems.at[lane, n, along],
                ).wait()
        part = None
        for xl in range(2):
            for q in range(2):
                term = lax.dot_general(
                    normed[q, 2 * down + xl],
                    ws[q, down, :, xl].reshape(KV, LANES),
                    (((1,), (1,)), ((), ())),
                    preferred_element_type=F32,
                )
                part = term if part is None else part + term
        pre[...] = jnp.where(n == 0, part, pre[...] + part)

    total = jnp.zeros((ROWS, HEAD), F32)
    cos, sin = both_halves(cosine, sine)
    for head in range(KV_HEADS):
        cols = slice(head * HEAD, (head + 1) * HEAD)
        values = pre[:, cols]
        keys[:, cols] = rotate(values, cos, sin).astype(BF16)
        total += values * dpre[:, cols].astype(F32)
    coef[...] = jnp.broadcast_to(jnp.sum(total, axis=1, keepdims=True) / D, (ROWS, 128))


def keys_call(core, y, z, normed, dpre, cosine, sine, pieces):
    return pl.pallas_call(
        keys_kernel,
        in_specs=[SMEM] * 3 + [VMEM] * 12,
        out_specs=[VMEM] * 3,
        out_shape=[
            jax.ShapeDtypeStruct((ROWS, KV), BF16),
            pltpu.VMEM((ROWS, 128), F32),
            pltpu.VMEM((2, 4, 2, 2, 4, 2, 32, LANES), BF16),
        ],
        scratch_shapes=[pltpu.VMEM((ROWS, KV), F32), pltpu.SemaphoreType.DMA((2, 4, 4))],
        compiler_params=params(12),
        cost_estimate=pl.CostEstimate(flops=2 * ROWS * D * KV, bytes_accessed=18 * MIB, transcendentals=0),
        name="keys",
    )(core, y, z, stay(normed), stay(dpre), cosine, sine, *map(stay, pieces))


def grad_kernel(normed, dpre, inv, coef, ws, grad):
    j = pl.program_id(0)
    for q in range(2):
        weights = ws[q, j // 2, :, j % 2].reshape(KV, LANES)
        back = jnp.dot(dpre[...], weights, preferred_element_type=F32)
        for k in range(LANES // 128):
            cols = slice(k * 128, (k + 1) * 128)
            into = slice(q * LANES + k * 128, q * LANES + (k + 1) * 128)
            less = normed[q, j, :, cols].astype(F32) * coef[...]
            grad[:, into] = ((back[:, cols] - less) * inv[...]).astype(BF16)


def grad_call(normed, dpre, inv, coef, ws):
    return pl.pallas_call(
        grad_kernel,
        grid=(STEPS,),
        in_specs=[VMEM] * 5,
        out_specs=pl.BlockSpec((ROWS, 2 * LANES), lambda j: (0, j)),
        out_shape=jax.ShapeDtypeStruct((ROWS, D), BF16),
        compiler_params=params(16),
        cost_estimate=pl.CostEstimate(flops=2 * ROWS * D * KV, bytes_accessed=18 * MIB, transcendentals=0),
        name="input_gradient",
    )(*map(stay, (normed, dpre, inv, coef, ws)))


def hop(value, first, second, distance):
    pairs = []
    for x in range(4):
        for y in range(4):
            for z in range(4):
                for core in range(2):
                    there = [x, y, z]
                    axis = first if core == 0 else second
                    there[axis] = (there[axis] + distance) % 4
                    pairs.append(tuple(flat(*at, core) for at in ((x, y, z), there)))
    return lax.ppermute(value, AXES, pairs)


def flat(x, y, z, core):
    return ((((x // 2) * 4 + y) * 2 + core) * 4 + z) * 2 + x % 2


def swap_cores(value):
    return lax.ppermute(value, "c", [(0, 1), (1, 0)])


X, Y, Z = 0, 1, 2


def shards(tokens, key_weight, cotangent):
    barrier = lax.optimization_barrier
    one = lambda value: value.astype(jnp.int32).reshape(1)
    index = lax.axis_index
    core, y, z, x = one(index("c")), one(index("y")), one(index("z")), one(index("xh") * 2 + index("xl"))
    first, odd, far = core[0] == 0, (x[0] & 1) == 1, (x[0] & 2) == 2
    cosine, sine = rope_tables((index("z") * 2 + index("xl")) * ROWS, ROWS)

    rows = key_weight.T
    left, right = rows[:, :LANES], rows[:, LANES:]
    came = swap_cores(jnp.where(first, right, left))
    pair = jnp.where(first, jnp.stack([left, came]), jnp.stack([came, right]))

    tokens, pair, core, y, z, x, first, odd, far, cosine, sine = barrier(
        (tokens, pair, core, y, z, x, first, odd, far, cosine, sine)
    )
    ring = [pair] + [hop(pair, X, X, -r) for r in (1, 2, 3)]
    prepared = prepare_call(0, tokens, cotangent, cosine, sine)
    for bit, step in ((odd, 1), (far, 2)):
        ring = [jnp.where(bit, ring[(i - step) % 4], ring[i]) for i in range(4)]
    near = jnp.stack(ring).reshape(2, 2, 2, 32, LANES)

    near, prepared = barrier((near, prepared))
    line = jnp.stack([near] + [hop(near, Y, Z, -r) for r in (1, 2, 3)])
    prepared = prepare_call(1, tokens, cotangent, cosine, sine, prepared)

    line, (normed, inv, dpre, dpre_t) = barrier((line, prepared))
    own = [line] + [hop(line, Z, Y, -r) for r in (1, 2, 3)]
    pieces = own + [swap_cores(piece) for piece in own]
    came = swap_cores(send_call(core, normed, dpre_t))
    cut = keep_call(core, x, y, z, normed, dpre_t, came)

    arrived = [[part[0]] + [hop(part[r], X, axis, r) for r in (1, 2, 3)] for part, axis in ((cut[:4], Y), (cut[4:], Z))]
    cut = [sum_first(core, y, second, parts) for parts, second in zip(arrived, (z, y))]
    arrived = [[part[0]] + [hop(part[r], Y, axis, r) for r in (1, 2, 3)] for part, axis in zip(cut, (Z, Y))]
    keys, coef, ws = keys_call(core, y, z, normed, dpre, cosine, sine, pieces)
    arrived, coef = barrier((arrived, coef))
    cut = sum_second(core, z, x, arrived[0] + arrived[1])
    arrived = [cut[0]] + [hop(cut[r], Z, X, r) for r in (1, 2, 3)]
    grad = grad_call(normed, dpre, inv, coef, ws)
    arrived, grad = barrier((arrived, grad))
    total = sum(part.astype(F32) for part in arrived) * (1.0 / 256.0)
    mine = jnp.where(first, total[0], total[1])
    came = swap_cores(jnp.where(first, total[1], total[0]))
    summed = jnp.where(
        first, jnp.concatenate([mine, came], 1), jnp.concatenate([came, mine], 1)
    )
    return keys, grad, summed.T


def solution(mesh):
    fine = Mesh(mesh.devices.reshape(2, 4, 2, 4, 2), AXES)
    rows = P(AXES, None)
    weight = P(("z", "xl"), ("xh", "y", "c"))
    return jax.shard_map(
        shards,
        mesh=fine,
        in_specs=(rows, weight, rows),
        out_specs=(rows, rows, weight),
        check_vma=False,
    )
```

```python
import math

import jax
import jax.numpy as jnp
from jax import lax
from jax.experimental import pallas as pl
from jax.experimental.pallas import tpu as pltpu
from jax.sharding import Mesh
from jax.sharding import PartitionSpec as P

HEAD = 128
KV_HEADS = 4
SEQ = 4096
EPS = 1e-05
D = 8192
KV = 512
ROWS = 512
LANES = 512
STEPS = D // (2 * LANES)
AXES = ("xh", "y", "c", "z", "xl")
MIB = 1 << 20
F32 = jnp.float32
BF16 = jnp.bfloat16


def rope_tables(start, count):
    position = ((start + jnp.arange(count, dtype=jnp.int32)) % SEQ).astype(F32)
    half = HEAD // 2
    inv_freq = jnp.exp(-math.log(10000.0) * jnp.arange(half, dtype=F32) / half)
    angle = position[:, None] * inv_freq[None, :]
    return jnp.cos(angle), jnp.sin(angle)


def both_halves(cosine, sine):
    cos, sin = cosine[...], sine[...]
    return jnp.concatenate([cos, cos], 1), jnp.concatenate([-sin, sin], 1)


def rotate(values, cosine, sine):
    return values * cosine + pltpu.roll(values, HEAD // 2, 1) * sine


def params(mib):
    return pltpu.CompilerParams(vmem_limit_bytes=mib * MIB)


SMEM = pl.BlockSpec(memory_space=pltpu.SMEM)


VMEM = pl.BlockSpec(memory_space=pltpu.VMEM)


def stay(value):
    return pltpu.with_memory_space_constraint(value, pltpu.VMEM)


def prepare_kernel(x, cot, cosine, sine, normed, inv, dpre, dpre_t):
    rows = pl.ds(pl.multiple_of(pl.program_id(0) * 128, 128), 128)
    acc = jnp.zeros((128, 128), F32)
    for k in range(D // 128):
        wide = x[:, k * 128 : (k + 1) * 128].astype(F32)
        acc += wide * wide
    scale = lax.rsqrt(jnp.sum(acc, axis=1, keepdims=True) / D + EPS)
    scale = jnp.broadcast_to(scale, (128, 128))
    inv[rows, :] = scale
    for k in range(D // 128):
        part, col = divmod(k * 128, LANES)
        value = x[:, k * 128 : (k + 1) * 128].astype(F32) * scale
        normed[part % 2, part // 2, rows, col : col + 128] = value.astype(BF16)
    cos, sin = both_halves(cosine, sine)
    for head in range(KV_HEADS):
        cols = slice(head * HEAD, (head + 1) * HEAD)
        turned = rotate(cot[:, cols].astype(F32), cos, -sin)
        dpre[rows, cols] = turned.astype(BF16)
        dpre_t[cols, rows] = turned.T.astype(BF16)


def prepare_call(tokens, cot, cosine, sine):
    rows = lambda width: pl.BlockSpec((128, width), lambda j: (j, 0))
    return pl.pallas_call(
        prepare_kernel,
        grid=(ROWS // 128,),
        in_specs=[rows(D), rows(KV), rows(HEAD // 2), rows(HEAD // 2)],
        out_specs=[VMEM] * 4,
        out_shape=[
            pltpu.VMEM((2, STEPS, ROWS, LANES), BF16),
            pltpu.VMEM((ROWS, 128), F32),
            pltpu.VMEM((ROWS, KV), BF16),
            pltpu.VMEM((KV, ROWS), BF16),
        ],
        compiler_params=params(16),
        cost_estimate=pl.CostEstimate(flops=10 * ROWS * D, bytes_accessed=18 * MIB, transcendentals=0),
        name="row_scales",
    )(
        pltpu.with_memory_space_constraint(tokens, pltpu.HBM),
        pltpu.with_memory_space_constraint(cot, pltpu.HBM),
        cosine,
        sine,
    )


def send_kernel(core, normed, dpre_t, out):
    @pl.loop(0, STEPS)
    def _(i):
        term = jnp.dot(dpre_t[...], normed[1 - core[0], i], preferred_element_type=F32)
        out[i] = term.astype(BF16).reshape(16, 32, LANES)


def send_call(core, normed, dpre_t):
    return pl.pallas_call(
        send_kernel,
        in_specs=[SMEM, VMEM, VMEM],
        out_specs=VMEM,
        out_shape=pltpu.VMEM((STEPS, 16, 32, LANES), BF16),
        compiler_params=params(8),
        cost_estimate=pl.CostEstimate(flops=ROWS * D * KV, bytes_accessed=9 * MIB, transcendentals=0),
        name="send_half",
    )(core, stay(normed), stay(dpre_t))


def keep_kernel(core, x, y, normed, dpre_t, came, *rest):
    (own, up, down, far_up, far_down), total = rest[:5], rest[5]

    @pl.loop(0, STEPS)
    def _(i):
        term = jnp.dot(dpre_t[...], normed[core[0], i], preferred_element_type=F32)
        total[i] = (term.reshape(16, 32, LANES) + came[i].astype(F32)).astype(BF16)

    first = core[0] == 0

    @pl.loop(0, 16)
    def _(n):
        a, b = n // 4, n % 4
        for r in range(4):
            x_at = jnp.where(first, (x[0] + r) % 4, a)
            y_at = jnp.where(first, a, (y[0] + r) % 4)
            block = total[2 * b + x_at % 2, pl.ds(8 * (x_at // 2) + 2 * y_at, 2)]
            if r != 2:
                {0: own, 1: up, 3: down}[r][a, b] = block
                continue

            @pl.when(a < 2)
            def _():
                far_up[a, b] = block

            @pl.when(a >= 2)
            def _():
                far_down[a - 2, b] = block


def keep_call(core, x, y, normed, dpre_t, came):
    part, half = (4, 4, 2, 32, LANES), (2, 4, 2, 32, LANES)
    return pl.pallas_call(
        keep_kernel,
        in_specs=[SMEM] * 3 + [VMEM] * 3,
        out_specs=[VMEM] * 5,
        out_shape=[pltpu.VMEM(part, BF16)] * 3 + [pltpu.VMEM(half, BF16)] * 2,
        scratch_shapes=[pltpu.VMEM((STEPS, 16, 32, LANES), BF16)],
        compiler_params=params(16),
        cost_estimate=pl.CostEstimate(flops=ROWS * D * KV, bytes_accessed=13 * MIB, transcendentals=0),
        name="keep_half",
    )(core, x, y, stay(normed), stay(dpre_t), stay(came))


def pass_on_kernel(up, down, from_below, from_above, up_out, down_out):
    up_out[:2] = (up[:2].astype(F32) + from_below[...].astype(F32)).astype(BF16)
    down_out[2:] = (down[2:].astype(F32) + from_above[...].astype(F32)).astype(BF16)


def pass_on(up, down, from_below, from_above):
    return pl.pallas_call(
        pass_on_kernel,
        in_specs=[VMEM] * 4,
        out_specs=[VMEM] * 2,
        out_shape=[pltpu.VMEM(up.shape, BF16)] * 2,
        input_output_aliases={0: 0, 1: 1},
        compiler_params=params(8),
        cost_estimate=pl.CostEstimate(flops=0, bytes_accessed=3 * MIB, transcendentals=0),
        name="pass_on",
    )(*map(stay, (up, down, from_below, from_above)))


def sum_cut_kernel(core, x, y, own, one, two, *outs):
    base = jnp.where(core[0] == 0, y[0], x[0])
    for r in range(4):
        k = (base + r) % 4
        total = own[k].astype(F32) + one[k].astype(F32) + two[k].astype(F32)
        outs[r][...] = total.astype(BF16)


def sum_cut(core, x, y, parts):
    shape = parts[0].shape
    return pl.pallas_call(
        sum_cut_kernel,
        in_specs=[SMEM] * 3 + [VMEM] * 3,
        out_specs=[VMEM] * 4,
        out_shape=[pltpu.VMEM(shape[1:], BF16)] * 4,
        compiler_params=params(8),
        cost_estimate=pl.CostEstimate(flops=64424509440, bytes_accessed=125829120, transcendentals=0),
        name="sum_first",
    )(core, x, y, *map(stay, parts))


def cut_kernel(z, one, two, three, four, *outs):
    for r in range(4):
        k = (z[0] + r) % 4
        total = one[k].astype(F32) + two[k].astype(F32)
        outs[r][...] = (total + three[k].astype(F32) + four[k].astype(F32)).astype(BF16)


def cut_call(z, parts):
    shape = parts[0].shape
    return pl.pallas_call(
        cut_kernel,
        in_specs=[SMEM] + [VMEM] * 4,
        out_specs=[VMEM] * 4,
        out_shape=[pltpu.VMEM(shape[1:], BF16)] * 4,
        compiler_params=params(8),
        cost_estimate=pl.CostEstimate(flops=0, bytes_accessed=2 * MIB, transcendentals=0),
        name="sum_second",
    )(z, *map(stay, parts))


def assemble_kernel(core, y, z, *refs):
    pieces, out = refs[:5], refs[5]
    for piece, r, start in zip(pieces, (0, 1, 3, 2, 2), (0, 0, 0, 0, 2)):

        @pl.loop(0, piece.shape[0])
        def _(i):
            k = i + start
            down, along = jnp.where(core[0] == 0, r, k), jnp.where(core[0] == 0, k, r)
            out[(z[0] + down) % 4, :, :, (y[0] + along) % 4] = piece[i]


def assemble(core, y, z, pieces):
    return pl.pallas_call(
        assemble_kernel,
        in_specs=[SMEM] * 3 + [VMEM] * 5,
        out_specs=VMEM,
        out_shape=pltpu.VMEM((4, 2, 2, 4, 2, 32, LANES), BF16),
        compiler_params=params(8),
        cost_estimate=pl.CostEstimate(flops=0, bytes_accessed=8 * MIB, transcendentals=0),
        name="assemble",
    )(core, y, z, *map(stay, pieces))


def products(half, normed, weights, pre):
    @pl.loop(0, 4)
    def _(n):
        part = None
        for xl in range(2):
            term = lax.dot_general(
                normed[half, 2 * n + xl],
                weights[n, :, xl].reshape(KV, LANES),
                (((1,), (1,)), ((), ())),
                preferred_element_type=F32,
            )
            part = term if part is None else part + term
        pre[...] += part


def own_kernel(core, normed, weights, pre):
    pre[...] = jnp.zeros_like(pre)
    products(core[0], normed, weights, pre)


def own_call(core, normed, weights):
    return pl.pallas_call(
        own_kernel,
        in_specs=[SMEM] + [VMEM] * 2,
        out_specs=VMEM,
        out_shape=pltpu.VMEM((ROWS, KV), F32),
        compiler_params=params(12),
        cost_estimate=pl.CostEstimate(flops=6442450944, bytes_accessed=12582912, transcendentals=0),
        name="keys_own_half",
    )(core, stay(normed), stay(weights))


def keys_kernel(core, normed, dpre, cosine, sine, weights, so_far, keys, coef, pre):
    pre[...] = so_far[...]
    products(1 - core[0], normed, weights, pre)
    total = jnp.zeros((ROWS, HEAD), F32)
    cos, sin = both_halves(cosine, sine)
    for head in range(KV_HEADS):
        cols = slice(head * HEAD, (head + 1) * HEAD)
        values = pre[:, cols]
        keys[:, cols] = rotate(values, cos, sin).astype(BF16)
        total += values * dpre[:, cols].astype(F32)
    coef[...] = jnp.broadcast_to(jnp.sum(total, axis=1, keepdims=True) / D, (ROWS, 128))


def keys_call(core, normed, dpre, cosine, sine, weights, so_far):
    return pl.pallas_call(
        keys_kernel,
        in_specs=[SMEM] + [VMEM] * 6,
        out_specs=[VMEM] * 2,
        out_shape=[
            jax.ShapeDtypeStruct((ROWS, KV), BF16),
            pltpu.VMEM((ROWS, 128), F32),
        ],
        scratch_shapes=[pltpu.VMEM((ROWS, KV), F32)],
        compiler_params=params(12),
        cost_estimate=pl.CostEstimate(flops=ROWS * D * KV, bytes_accessed=9 * MIB, transcendentals=0),
        name="keys",
    )(core, stay(normed), stay(dpre), cosine, sine, stay(weights), stay(so_far))


def grad_kernel(core, normed, dpre, inv, coef, own, other, grad):
    j = pl.program_id(0)
    for half, weights in ((core[0], own), (1 - core[0], other)):
        here = weights[j // 2, :, j % 2].reshape(KV, LANES)
        back = jnp.dot(dpre[...], here, preferred_element_type=F32)
        for k in range(LANES // 128):
            cols = slice(k * 128, (k + 1) * 128)
            into = pl.ds(pl.multiple_of(half * LANES + k * 128, 128), 128)
            less = normed[half, j, :, cols].astype(F32) * coef[...]
            grad[:, into] = ((back[:, cols] - less) * inv[...]).astype(BF16)


def grad_call(core, normed, dpre, inv, coef, own, other):
    return pl.pallas_call(
        grad_kernel,
        grid=(STEPS,),
        in_specs=[SMEM] + [VMEM] * 6,
        out_specs=pl.BlockSpec((ROWS, 2 * LANES), lambda j: (0, j)),
        out_shape=jax.ShapeDtypeStruct((ROWS, D), BF16),
        compiler_params=params(16),
        cost_estimate=pl.CostEstimate(flops=2 * ROWS * D * KV, bytes_accessed=18 * MIB, transcendentals=0),
        name="input_gradient",
    )(core, *map(stay, (normed, dpre, inv, coef, own, other)))


def hop(value, first, second, distance):
    pairs = []
    for x in range(4):
        for y in range(4):
            for z in range(4):
                for core in range(2):
                    there = [x, y, z]
                    axis = first if core == 0 else second
                    there[axis] = (there[axis] + distance) % 4
                    pairs.append(tuple(flat(*at, core) for at in ((x, y, z), there)))
    return lax.ppermute(value, AXES, pairs)


def flat(x, y, z, core):
    return ((((x // 2) * 4 + y) * 2 + core) * 4 + z) * 2 + x % 2


def swap_cores(value):
    return lax.ppermute(value, "c", [(0, 1), (1, 0)])


X, Y, Z = 0, 1, 2


def shards(tokens, key_weight, cotangent):
    barrier = lax.optimization_barrier
    one = lambda value: value.astype(jnp.int32).reshape(1)
    index = lax.axis_index
    core, y, z, x = one(index("c")), one(index("y")), one(index("z")), one(index("xh") * 2 + index("xl"))
    first, odd, far = core[0] == 0, (x[0] & 1) == 1, (x[0] & 2) == 2
    cosine, sine = rope_tables((index("z") * 2 + index("xl")) * ROWS, ROWS)

    rows = key_weight.T
    left, right = rows[:, :LANES], rows[:, LANES:]
    came = swap_cores(jnp.where(first, right, left))
    pair = jnp.where(first, jnp.stack([left, came]), jnp.stack([came, right]))

    tokens, pair, core, y, z, x, first, odd, far, cosine, sine = barrier(
        (tokens, pair, core, y, z, x, first, odd, far, cosine, sine)
    )
    ring = [pair] + [hop(pair, X, X, -r) for r in (1, 2, 3)]
    normed, inv, dpre, dpre_t = prepare_call(tokens, cotangent, cosine, sine)
    for bit, step in ((odd, 1), (far, 2)):
        ring = [jnp.where(bit, ring[(i - step) % 4], ring[i]) for i in range(4)]
    near = jnp.stack(ring).reshape(2, 2, 2, 32, LANES)

    near, normed = barrier((near, normed))
    line = jnp.stack([near] + [hop(near, Y, Z, -r) for r in (1, 2, 3)])
    send = send_call(core, normed, dpre_t)

    line, send = barrier((line, send))
    above, below = hop(line, Z, Y, -1), hop(line, Z, Y, 1)
    came = swap_cores(send)
    own, up, down, far_up, far_down = keep_call(core, x, y, normed, dpre_t, came)

    from_below, from_above = hop(far_up, X, Y, 1), hop(far_down, X, Y, -1)
    above, below = barrier((above, below, own))[:2]
    across = hop(above[:2], Z, Y, -1), hop(below[2:], Z, Y, 1)
    up, down = pass_on(up, down, from_below, from_above)
    arrived = [own, hop(up, X, Y, 1), hop(down, X, Y, -1)]
    weights = assemble(core, y, z, [line, above, below, across[0], across[1]])
    so_far = own_call(core, normed, weights)
    others = swap_cores(barrier((weights, so_far))[0])
    keys, coef = keys_call(core, normed, dpre, cosine, sine, others, so_far)
    cut = sum_cut(core, x, y, arrived)
    arrived = [cut[0]] + [hop(cut[r], Y, X, r) for r in (2, 1, 3)]
    arrived, coef = barrier((arrived, coef))
    cut = cut_call(z, arrived)
    arrived = [cut[0]] + [hop(cut[r], Z, Z, r) for r in (2, 1, 3)]
    grad = grad_call(core, normed, dpre, inv, coef, weights, others)
    arrived, grad = barrier((arrived, grad))
    total = sum(part.astype(F32) for part in arrived) * (1.0 / 256.0)
    mine = jnp.where(first, total[0], total[1])
    came = swap_cores(jnp.where(first, total[1], total[0]))
    summed = jnp.where(
        first, jnp.concatenate([mine, came], 1), jnp.concatenate([came, mine], 1)
    )
    return keys, grad, summed.T


def solution(mesh):
    fine = Mesh(mesh.devices.reshape(2, 4, 2, 4, 2), AXES)
    rows = P(AXES, None)
    weight = P(("z", "xl"), ("xh", "y", "c"))
    return jax.shard_map(
        shards,
        mesh=fine,
        in_specs=(rows, weight, rows),
        out_specs=(rows, rows, weight),
        check_vma=False,
    )
```

```python
import math

import jax
import jax.numpy as jnp
from jax import lax
from jax.experimental import pallas as pl
from jax.experimental.pallas import tpu as pltpu
from jax.sharding import Mesh
from jax.sharding import PartitionSpec as P

HEAD = 128
KV_HEADS = 4
SEQ = 4096
EPS = 1e-05
D = 8192
KV = 512
ROWS = 512
LANES = 512
STEPS = D // (2 * LANES)
AXES = ("xh", "y", "c", "z", "xl")
MIB = 1 << 20
F32 = jnp.float32
BF16 = jnp.bfloat16


def rope_tables(start, count):
    position = ((start + jnp.arange(count, dtype=jnp.int32)) % SEQ).astype(F32)
    half = HEAD // 2
    inv_freq = jnp.exp(-math.log(10000.0) * jnp.arange(half, dtype=F32) / half)
    angle = position[:, None] * inv_freq[None, :]
    return jnp.cos(angle), jnp.sin(angle)


def both_halves(cosine, sine):
    cos, sin = cosine[...], sine[...]
    return jnp.concatenate([cos, cos], 1), jnp.concatenate([-sin, sin], 1)


def rotate(values, cosine, sine):
    return values * cosine + pltpu.roll(values, HEAD // 2, 1) * sine


def params(mib):
    return pltpu.CompilerParams(vmem_limit_bytes=mib * MIB)


SMEM = pl.BlockSpec(memory_space=pltpu.SMEM)


VMEM = pl.BlockSpec(memory_space=pltpu.VMEM)


def stay(value):
    return pltpu.with_memory_space_constraint(value, pltpu.VMEM)


def prepare_kernel(x, cot, cosine, sine, normed, inv, dpre, dpre_t):
    rows = pl.ds(pl.multiple_of(pl.program_id(0) * 128, 128), 128)
    acc = jnp.zeros((128, 128), F32)
    for k in range(D // 128):
        wide = x[:, k * 128 : (k + 1) * 128].astype(F32)
        acc += wide * wide
    scale = lax.rsqrt(jnp.sum(acc, axis=1, keepdims=True) / D + EPS)
    scale = jnp.broadcast_to(scale, (128, 128))
    inv[rows, :] = scale
    for k in range(D // 128):
        part, col = divmod(k * 128, LANES)
        value = x[:, k * 128 : (k + 1) * 128].astype(F32) * scale
        normed[part % 2, part // 2, rows, col : col + 128] = value.astype(BF16)
    cos, sin = both_halves(cosine, sine)
    for head in range(KV_HEADS):
        cols = slice(head * HEAD, (head + 1) * HEAD)
        turned = rotate(cot[:, cols].astype(F32), cos, -sin)
        dpre[rows, cols] = turned.astype(BF16)
        dpre_t[cols, rows] = turned.T.astype(BF16)


def prepare_call(tokens, cot, cosine, sine):
    rows = lambda width: pl.BlockSpec((128, width), lambda j: (j, 0))
    return pl.pallas_call(
        prepare_kernel,
        grid=(ROWS // 128,),
        in_specs=[rows(D), rows(KV), rows(HEAD // 2), rows(HEAD // 2)],
        out_specs=[VMEM] * 4,
        out_shape=[
            pltpu.VMEM((2, STEPS, ROWS, LANES), BF16),
            pltpu.VMEM((ROWS, 128), F32),
            pltpu.VMEM((ROWS, KV), BF16),
            pltpu.VMEM((KV, ROWS), BF16),
        ],
        compiler_params=params(16),
        cost_estimate=pl.CostEstimate(flops=10 * ROWS * D, bytes_accessed=18 * MIB, transcendentals=0),
        name="row_scales",
    )(
        pltpu.with_memory_space_constraint(tokens, pltpu.HBM),
        pltpu.with_memory_space_constraint(cot, pltpu.HBM),
        cosine,
        sine,
    )


def terms_call(core, normed, dpre_t, other):
    def kernel(core, normed, dpre_t, out):
        half = 1 - core[0] if other else core[0]

        @pl.loop(0, STEPS)
        def _(i):
            term = jnp.dot(dpre_t[...], normed[half, i], preferred_element_type=F32)
            out[i] = term.astype(BF16).reshape(16, 32, LANES)

    return pl.pallas_call(
        kernel,
        in_specs=[SMEM, VMEM, VMEM],
        out_specs=VMEM,
        out_shape=pltpu.VMEM((STEPS, 16, 32, LANES), BF16),
        compiler_params=params(8),
        cost_estimate=pl.CostEstimate(flops=ROWS * D * KV, bytes_accessed=9 * MIB, transcendentals=0),
        name="send_half" if other else "keep_half",
    )(core, stay(normed), stay(dpre_t))


def add_kernel(core, x, y, kept, came, own, up, down, far_up, far_down):
    first = core[0] == 0

    @pl.loop(0, 16)
    def _(n):
        a, b = n // 4, n % 4
        for r in range(4):
            x_at = jnp.where(first, (x[0] + r) % 4, a)
            y_at = jnp.where(first, a, (y[0] + r) % 4)
            at = (2 * b + x_at % 2, pl.ds(8 * (x_at // 2) + 2 * y_at, 2))
            block = kept[at] + came[at]
            if r != 2:
                {0: own, 1: up, 3: down}[r][a, b] = block
                continue

            @pl.when(a < 2)
            def _():
                far_up[a, b] = block

            @pl.when(a >= 2)
            def _():
                far_down[a - 2, b] = block


def add_call(core, x, y, kept, came):
    part, half = (4, 4, 2, 32, LANES), (2, 4, 2, 32, LANES)
    return pl.pallas_call(
        add_kernel,
        in_specs=[SMEM] * 3 + [VMEM] * 2,
        out_specs=[VMEM] * 5,
        out_shape=[pltpu.VMEM(part, BF16)] * 3 + [pltpu.VMEM(half, BF16)] * 2,
        compiler_params=params(16),
        cost_estimate=pl.CostEstimate(flops=0, bytes_accessed=12 * MIB, transcendentals=0),
        name="add_cores",
    )(core, x, y, stay(kept), stay(came))


def pass_on_kernel(up, down, from_below, from_above, up_out, down_out):
    up_out[:2] = (up[:2].astype(F32) + from_below[...].astype(F32)).astype(BF16)
    down_out[2:] = (down[2:].astype(F32) + from_above[...].astype(F32)).astype(BF16)


def pass_on(up, down, from_below, from_above):
    return pl.pallas_call(
        pass_on_kernel,
        in_specs=[VMEM] * 4,
        out_specs=[VMEM] * 2,
        out_shape=[pltpu.VMEM(up.shape, BF16)] * 2,
        input_output_aliases={0: 0, 1: 1},
        compiler_params=params(8),
        cost_estimate=pl.CostEstimate(flops=0, bytes_accessed=3 * MIB, transcendentals=0),
        name="pass_on",
    )(*map(stay, (up, down, from_below, from_above)))


def sum_cut_kernel(core, x, y, own, one, two, *outs):
    base = jnp.where(core[0] == 0, y[0], x[0])
    for r in range(4):
        k = (base + r) % 4
        total = own[k].astype(F32) + one[k].astype(F32) + two[k].astype(F32)
        outs[r][...] = total.astype(BF16)


def sum_cut(core, x, y, parts):
    shape = parts[0].shape
    return pl.pallas_call(
        sum_cut_kernel,
        in_specs=[SMEM] * 3 + [VMEM] * 3,
        out_specs=[VMEM] * 4,
        out_shape=[pltpu.VMEM(shape[1:], BF16)] * 4,
        compiler_params=params(8),
        cost_estimate=pl.CostEstimate(flops=64424509440, bytes_accessed=125829120, transcendentals=0),
        name="sum_first",
    )(core, x, y, *map(stay, parts))


def cut_kernel(z, one, two, three, four, *outs):
    for r in range(4):
        k = (z[0] + r) % 4
        total = one[k].astype(F32) + two[k].astype(F32)
        outs[r][...] = (total + three[k].astype(F32) + four[k].astype(F32)).astype(BF16)


def cut_call(z, parts):
    shape = parts[0].shape
    return pl.pallas_call(
        cut_kernel,
        in_specs=[SMEM] + [VMEM] * 4,
        out_specs=[VMEM] * 4,
        out_shape=[pltpu.VMEM(shape[1:], BF16)] * 4,
        compiler_params=params(8),
        cost_estimate=pl.CostEstimate(flops=0, bytes_accessed=2 * MIB, transcendentals=0),
        name="sum_second",
    )(z, *map(stay, parts))


def assemble_kernel(core, y, z, *refs):
    pieces, out = refs[:5], refs[5]
    for piece, r, start in zip(pieces, (0, 1, 3, 2, 2), (0, 0, 0, 0, 2)):

        @pl.loop(0, piece.shape[0])
        def _(i):
            k = i + start
            down, along = jnp.where(core[0] == 0, r, k), jnp.where(core[0] == 0, k, r)
            out[(z[0] + down) % 4, :, :, (y[0] + along) % 4] = piece[i]


def assemble(core, y, z, pieces):
    return pl.pallas_call(
        assemble_kernel,
        in_specs=[SMEM] * 3 + [VMEM] * 5,
        out_specs=VMEM,
        out_shape=pltpu.VMEM((4, 2, 2, 4, 2, 32, LANES), BF16),
        compiler_params=params(8),
        cost_estimate=pl.CostEstimate(flops=0, bytes_accessed=8 * MIB, transcendentals=0),
        name="assemble",
    )(core, y, z, *map(stay, pieces))


def products(half, normed, weights, pre):
    @pl.loop(0, 4)
    def _(n):
        part = None
        for xl in range(2):
            term = lax.dot_general(
                normed[half, 2 * n + xl],
                weights[n, :, xl].reshape(KV, LANES),
                (((1,), (1,)), ((), ())),
                preferred_element_type=F32,
            )
            part = term if part is None else part + term
        pre[...] += part


def own_kernel(core, normed, weights, pre):
    pre[...] = jnp.zeros_like(pre)
    products(core[0], normed, weights, pre)


def own_call(core, normed, weights):
    return pl.pallas_call(
        own_kernel,
        in_specs=[SMEM] + [VMEM] * 2,
        out_specs=VMEM,
        out_shape=pltpu.VMEM((ROWS, KV), F32),
        compiler_params=params(12),
        cost_estimate=pl.CostEstimate(flops=6442450944, bytes_accessed=12582912, transcendentals=0),
        name="keys_own_half",
    )(core, stay(normed), stay(weights))


def keys_kernel(core, normed, dpre, cosine, sine, weights, so_far, keys, coef, pre):
    pre[...] = so_far[...]
    products(1 - core[0], normed, weights, pre)
    total = jnp.zeros((ROWS, HEAD), F32)
    cos, sin = both_halves(cosine, sine)
    for head in range(KV_HEADS):
        cols = slice(head * HEAD, (head + 1) * HEAD)
        values = pre[:, cols]
        keys[:, cols] = rotate(values, cos, sin).astype(BF16)
        total += values * dpre[:, cols].astype(F32)
    coef[...] = jnp.broadcast_to(jnp.sum(total, axis=1, keepdims=True) / D, (ROWS, 128))


def keys_call(core, normed, dpre, cosine, sine, weights, so_far):
    return pl.pallas_call(
        keys_kernel,
        in_specs=[SMEM] + [VMEM] * 6,
        out_specs=[VMEM] * 2,
        out_shape=[
            jax.ShapeDtypeStruct((ROWS, KV), BF16),
            pltpu.VMEM((ROWS, 128), F32),
        ],
        scratch_shapes=[pltpu.VMEM((ROWS, KV), F32)],
        compiler_params=params(12),
        cost_estimate=pl.CostEstimate(flops=ROWS * D * KV, bytes_accessed=9 * MIB, transcendentals=0),
        name="keys",
    )(core, stay(normed), stay(dpre), cosine, sine, stay(weights), stay(so_far))


def grad_kernel(core, normed, dpre, inv, coef, own, other, grad):
    j = pl.program_id(0)
    for half, weights in ((core[0], own), (1 - core[0], other)):
        here = weights[j // 2, :, j % 2].reshape(KV, LANES)
        back = jnp.dot(dpre[...], here, preferred_element_type=F32)
        for k in range(LANES // 128):
            cols = slice(k * 128, (k + 1) * 128)
            into = pl.ds(pl.multiple_of(half * LANES + k * 128, 128), 128)
            less = normed[half, j, :, cols].astype(F32) * coef[...]
            grad[:, into] = ((back[:, cols] - less) * inv[...]).astype(BF16)


def grad_call(core, normed, dpre, inv, coef, own, other):
    return pl.pallas_call(
        grad_kernel,
        grid=(STEPS,),
        in_specs=[SMEM] + [VMEM] * 6,
        out_specs=pl.BlockSpec((ROWS, 2 * LANES), lambda j: (0, j)),
        out_shape=jax.ShapeDtypeStruct((ROWS, D), BF16),
        compiler_params=params(16),
        cost_estimate=pl.CostEstimate(flops=2 * ROWS * D * KV, bytes_accessed=18 * MIB, transcendentals=0),
        name="input_gradient",
    )(core, *map(stay, (normed, dpre, inv, coef, own, other)))


def hop(value, first, second, distance):
    pairs = []
    for x in range(4):
        for y in range(4):
            for z in range(4):
                for core in range(2):
                    there = [x, y, z]
                    axis = first if core == 0 else second
                    there[axis] = (there[axis] + distance) % 4
                    pairs.append(tuple(flat(*at, core) for at in ((x, y, z), there)))
    return lax.ppermute(value, AXES, pairs)


def flat(x, y, z, core):
    return ((((x // 2) * 4 + y) * 2 + core) * 4 + z) * 2 + x % 2


def swap_cores(value):
    return lax.ppermute(value, "c", [(0, 1), (1, 0)])


X, Y, Z = 0, 1, 2


def shards(tokens, key_weight, cotangent):
    barrier = lax.optimization_barrier
    one = lambda value: value.astype(jnp.int32).reshape(1)
    index = lax.axis_index
    core, y, z, x = one(index("c")), one(index("y")), one(index("z")), one(index("xh") * 2 + index("xl"))
    first, odd, far = core[0] == 0, (x[0] & 1) == 1, (x[0] & 2) == 2
    cosine, sine = rope_tables((index("z") * 2 + index("xl")) * ROWS, ROWS)

    rows = key_weight.T
    left, right = rows[:, :LANES], rows[:, LANES:]
    came = swap_cores(jnp.where(first, right, left))
    pair = jnp.where(first, jnp.stack([left, came]), jnp.stack([came, right]))

    tokens, pair, core, y, z, x, first, odd, far, cosine, sine = barrier(
        (tokens, pair, core, y, z, x, first, odd, far, cosine, sine)
    )
    ring = [pair] + [hop(pair, X, X, -r) for r in (1, 2, 3)]
    normed, inv, dpre, dpre_t = prepare_call(tokens, cotangent, cosine, sine)
    for bit, step in ((odd, 1), (far, 2)):
        ring = [jnp.where(bit, ring[(i - step) % 4], ring[i]) for i in range(4)]
    near = jnp.stack(ring).reshape(2, 2, 2, 32, LANES)

    near, normed = barrier((near, normed))
    line = jnp.stack([near] + [hop(near, Y, Z, -r) for r in (1, 2, 3)])
    send = terms_call(core, normed, dpre_t, True)

    line, send = barrier((line, send))
    above, below = hop(line, Z, Y, -1), hop(line, Z, Y, 1)
    came = swap_cores(send)
    kept = terms_call(core, normed, dpre_t, False)
    own, up, down, far_up, far_down = add_call(core, x, y, kept, came)

    from_below, from_above = hop(far_up, X, Y, 1), hop(far_down, X, Y, -1)
    above, below = barrier((above, below, own))[:2]
    across = hop(above[:2], Z, Y, -1), hop(below[2:], Z, Y, 1)
    up, down = pass_on(up, down, from_below, from_above)
    arrived = [own, hop(up, X, Y, 1), hop(down, X, Y, -1)]
    weights = assemble(core, y, z, [line, above, below, across[0], across[1]])
    so_far = own_call(core, normed, weights)
    others = swap_cores(barrier((weights, so_far))[0])
    keys, coef = keys_call(core, normed, dpre, cosine, sine, others, so_far)
    cut = sum_cut(core, x, y, arrived)
    arrived = [cut[0]] + [hop(cut[r], Y, X, r) for r in (2, 1, 3)]
    arrived, coef = barrier((arrived, coef))
    cut = cut_call(z, arrived)
    arrived = [cut[0]] + [hop(cut[r], Z, Z, r) for r in (2, 1, 3)]
    grad = grad_call(core, normed, dpre, inv, coef, weights, others)
    arrived, grad = barrier((arrived, grad))
    total = sum(part.astype(F32) for part in arrived) * (1.0 / 256.0)
    mine = jnp.where(first, total[0], total[1])
    came = swap_cores(jnp.where(first, total[1], total[0]))
    summed = jnp.where(
        first, jnp.concatenate([mine, came], 1), jnp.concatenate([came, mine], 1)
    )
    return keys, grad, summed.T


def solution(mesh):
    fine = Mesh(mesh.devices.reshape(2, 4, 2, 4, 2), AXES)
    rows = P(AXES, None)
    weight = P(("z", "xl"), ("xh", "y", "c"))
    return jax.shard_map(
        shards,
        mesh=fine,
        in_specs=(rows, weight, rows),
        out_specs=(rows, rows, weight),
        check_vma=False,
    )
```

```python
import math

import jax
import jax.numpy as jnp
from jax import lax
from jax.experimental import pallas as pl
from jax.experimental.pallas import tpu as pltpu
from jax.sharding import Mesh
from jax.sharding import PartitionSpec as P

HEAD = 128
KV_HEADS = 4
SEQ = 4096
EPS = 1e-05
D = 8192
KV = 512
ROWS = 512
LANES = 512
STEPS = D // (2 * LANES)
AXES = ("xh", "y", "c", "z", "xl")
MIB = 1 << 20
F32 = jnp.float32
BF16 = jnp.bfloat16


def rope_tables(start, count):
    position = ((start + jnp.arange(count, dtype=jnp.int32)) % SEQ).astype(F32)
    half = HEAD // 2
    inv_freq = jnp.exp(-math.log(10000.0) * jnp.arange(half, dtype=F32) / half)
    angle = position[:, None] * inv_freq[None, :]
    return jnp.cos(angle), jnp.sin(angle)


def both_halves(cosine, sine):
    cos, sin = cosine[...], sine[...]
    return jnp.concatenate([cos, cos], 1), jnp.concatenate([-sin, sin], 1)


def rotate(values, cosine, sine):
    return values * cosine + pltpu.roll(values, HEAD // 2, 1) * sine


def params(mib):
    return pltpu.CompilerParams(vmem_limit_bytes=mib * MIB)


SMEM = pl.BlockSpec(memory_space=pltpu.SMEM)


VMEM = pl.BlockSpec(memory_space=pltpu.VMEM)


def stay(value):
    return pltpu.with_memory_space_constraint(value, pltpu.VMEM)


def prepare_kernel(x, cot, cosine, sine, normed, inv, dpre, dpre_t):
    rows = pl.ds(pl.multiple_of(pl.program_id(0) * 128, 128), 128)
    acc = jnp.zeros((128, 128), F32)
    for k in range(D // 128):
        wide = x[:, k * 128 : (k + 1) * 128].astype(F32)
        acc += wide * wide
    scale = lax.rsqrt(jnp.sum(acc, axis=1, keepdims=True) / D + EPS)
    scale = jnp.broadcast_to(scale, (128, 128))
    inv[rows, :] = scale
    for k in range(D // 128):
        part, col = divmod(k * 128, LANES)
        value = x[:, k * 128 : (k + 1) * 128].astype(F32) * scale
        normed[part % 2, part // 2, rows, col : col + 128] = value.astype(BF16)
    cos, sin = both_halves(cosine, sine)
    for head in range(KV_HEADS):
        cols = slice(head * HEAD, (head + 1) * HEAD)
        turned = rotate(cot[:, cols].astype(F32), cos, -sin)
        dpre[rows, cols] = turned.astype(BF16)
        dpre_t[cols, rows] = turned.T.astype(BF16)


def prepare_call(tokens, cot, cosine, sine):
    rows = lambda width: pl.BlockSpec((128, width), lambda j: (j, 0))
    return pl.pallas_call(
        prepare_kernel,
        grid=(ROWS // 128,),
        in_specs=[rows(D), rows(KV), rows(HEAD // 2), rows(HEAD // 2)],
        out_specs=[VMEM] * 4,
        out_shape=[
            pltpu.VMEM((2, STEPS, ROWS, LANES), BF16),
            pltpu.VMEM((ROWS, 128), F32),
            pltpu.VMEM((ROWS, KV), BF16),
            pltpu.VMEM((KV, ROWS), BF16),
        ],
        compiler_params=params(16),
        cost_estimate=pl.CostEstimate(flops=10 * ROWS * D, bytes_accessed=18 * MIB, transcendentals=0),
        name="row_scales",
    )(
        pltpu.with_memory_space_constraint(tokens, pltpu.HBM),
        pltpu.with_memory_space_constraint(cot, pltpu.HBM),
        cosine,
        sine,
    )


def terms_call(core, normed, dpre_t, other):
    def kernel(core, normed, dpre_t, out):
        half = 1 - core[0] if other else core[0]

        @pl.loop(0, STEPS)
        def _(i):
            term = jnp.dot(dpre_t[...], normed[half, i], preferred_element_type=F32)
            out[i] = term.astype(BF16).reshape(16, 32, LANES)

    return pl.pallas_call(
        kernel,
        in_specs=[SMEM, VMEM, VMEM],
        out_specs=VMEM,
        out_shape=pltpu.VMEM((STEPS, 16, 32, LANES), BF16),
        compiler_params=params(8),
        cost_estimate=pl.CostEstimate(flops=ROWS * D * KV, bytes_accessed=9 * MIB, transcendentals=0),
        name="send_half" if other else "keep_half",
    )(core, stay(normed), stay(dpre_t))


def add_kernel(core, x, y, kept, came, own, up, down, far_up, far_down):
    first = core[0] == 0

    @pl.loop(0, 16)
    def _(n):
        a, b = n // 4, n % 4
        for r in range(4):
            x_at = jnp.where(first, (x[0] + r) % 4, a)
            y_at = jnp.where(first, a, (y[0] + r) % 4)
            at = (2 * b + x_at % 2, pl.ds(8 * (x_at // 2) + 2 * y_at, 2))
            block = kept[at] + came[at]
            if r != 2:
                {0: own, 1: up, 3: down}[r][a, b] = block
                continue

            @pl.when(a < 2)
            def _():
                far_up[a, b] = block

            @pl.when(a >= 2)
            def _():
                far_down[a - 2, b] = block


def add_call(core, x, y, kept, came):
    part, half = (4, 4, 2, 32, LANES), (2, 4, 2, 32, LANES)
    return pl.pallas_call(
        add_kernel,
        in_specs=[SMEM] * 3 + [VMEM] * 2,
        out_specs=[VMEM] * 5,
        out_shape=[pltpu.VMEM(part, BF16)] * 3 + [pltpu.VMEM(half, BF16)] * 2,
        compiler_params=params(16),
        cost_estimate=pl.CostEstimate(flops=0, bytes_accessed=12 * MIB, transcendentals=0),
        name="add_cores",
    )(core, x, y, stay(kept), stay(came))


def pass_on_kernel(up, down, from_below, from_above, up_out, down_out):
    up_out[:2] = (up[:2].astype(F32) + from_below[...].astype(F32)).astype(BF16)
    down_out[2:] = (down[2:].astype(F32) + from_above[...].astype(F32)).astype(BF16)


def pass_on(up, down, from_below, from_above):
    return pl.pallas_call(
        pass_on_kernel,
        in_specs=[VMEM] * 4,
        out_specs=[VMEM] * 2,
        out_shape=[pltpu.VMEM(up.shape, BF16)] * 2,
        input_output_aliases={0: 0, 1: 1},
        compiler_params=params(8),
        cost_estimate=pl.CostEstimate(flops=0, bytes_accessed=3 * MIB, transcendentals=0),
        name="pass_on",
    )(*map(stay, (up, down, from_below, from_above)))


def sum_cut_kernel(core, x, y, own, one, two, *outs):
    base = jnp.where(core[0] == 0, y[0], x[0])
    for r in range(4):
        k = (base + r) % 4
        total = own[k].astype(F32) + one[k].astype(F32) + two[k].astype(F32)
        outs[r][...] = total.astype(BF16)


def sum_cut(core, x, y, parts):
    shape = parts[0].shape
    return pl.pallas_call(
        sum_cut_kernel,
        in_specs=[SMEM] * 3 + [VMEM] * 3,
        out_specs=[VMEM] * 4,
        out_shape=[pltpu.VMEM(shape[1:], BF16)] * 4,
        compiler_params=params(8),
        cost_estimate=pl.CostEstimate(flops=64424509440, bytes_accessed=125829120, transcendentals=0),
        name="sum_first",
    )(core, x, y, *map(stay, parts))


def cut_kernel(z, one, two, three, four, *outs):
    for r in range(4):
        k = (z[0] + r) % 4
        total = one[k].astype(F32) + two[k].astype(F32)
        outs[r][...] = (total + three[k].astype(F32) + four[k].astype(F32)).astype(BF16)


def cut_call(z, parts):
    shape = parts[0].shape
    return pl.pallas_call(
        cut_kernel,
        in_specs=[SMEM] + [VMEM] * 4,
        out_specs=[VMEM] * 4,
        out_shape=[pltpu.VMEM(shape[1:], BF16)] * 4,
        compiler_params=params(8),
        cost_estimate=pl.CostEstimate(flops=0, bytes_accessed=2 * MIB, transcendentals=0),
        name="sum_second",
    )(z, *map(stay, parts))


def assemble_kernel(core, y, z, *refs):
    pieces, out = refs[:5], refs[5]
    for piece, r, start in zip(pieces, (0, 1, 3, 2, 2), (0, 0, 0, 0, 2)):

        @pl.loop(0, piece.shape[0])
        def _(i):
            k = i + start
            down, along = jnp.where(core[0] == 0, r, k), jnp.where(core[0] == 0, k, r)
            out[(z[0] + down) % 4, :, :, (y[0] + along) % 4] = piece[i]


def assemble(core, y, z, pieces):
    return pl.pallas_call(
        assemble_kernel,
        in_specs=[SMEM] * 3 + [VMEM] * 5,
        out_specs=VMEM,
        out_shape=pltpu.VMEM((4, 2, 2, 4, 2, 32, LANES), BF16),
        compiler_params=params(8),
        cost_estimate=pl.CostEstimate(flops=0, bytes_accessed=8 * MIB, transcendentals=0),
        name="assemble",
    )(core, y, z, *map(stay, pieces))


def products(half, normed, weights, pre):
    @pl.loop(0, 4)
    def _(n):
        part = None
        for xl in range(2):
            term = lax.dot_general(
                normed[half, 2 * n + xl],
                weights[n, :, xl].reshape(KV, LANES),
                (((1,), (1,)), ((), ())),
                preferred_element_type=F32,
            )
            part = term if part is None else part + term
        pre[...] += part


def own_kernel(core, normed, weights, pre):
    pre[...] = jnp.zeros_like(pre)
    products(core[0], normed, weights, pre)


def own_call(core, normed, weights):
    return pl.pallas_call(
        own_kernel,
        in_specs=[SMEM] + [VMEM] * 2,
        out_specs=VMEM,
        out_shape=pltpu.VMEM((ROWS, KV), F32),
        compiler_params=params(12),
        cost_estimate=pl.CostEstimate(flops=6442450944, bytes_accessed=12582912, transcendentals=0),
        name="keys_own_half",
    )(core, stay(normed), stay(weights))


def keys_kernel(core, normed, dpre, cosine, sine, weights, so_far, keys, coef, pre):
    pre[...] = so_far[...]
    products(1 - core[0], normed, weights, pre)
    total = jnp.zeros((ROWS, HEAD), F32)
    cos, sin = both_halves(cosine, sine)
    for head in range(KV_HEADS):
        cols = slice(head * HEAD, (head + 1) * HEAD)
        values = pre[:, cols]
        keys[:, cols] = rotate(values, cos, sin).astype(BF16)
        total += values * dpre[:, cols].astype(F32)
    coef[...] = jnp.broadcast_to(jnp.sum(total, axis=1, keepdims=True) / D, (ROWS, 128))


def keys_call(core, normed, dpre, cosine, sine, weights, so_far):
    return pl.pallas_call(
        keys_kernel,
        in_specs=[SMEM] + [VMEM] * 6,
        out_specs=[VMEM] * 2,
        out_shape=[
            jax.ShapeDtypeStruct((ROWS, KV), BF16),
            pltpu.VMEM((ROWS, 128), F32),
        ],
        scratch_shapes=[pltpu.VMEM((ROWS, KV), F32)],
        compiler_params=params(12),
        cost_estimate=pl.CostEstimate(flops=ROWS * D * KV, bytes_accessed=9 * MIB, transcendentals=0),
        name="keys",
    )(core, stay(normed), stay(dpre), cosine, sine, stay(weights), stay(so_far))


def grad_kernel(core, normed, dpre, inv, coef, own, other, grad):
    for t in range(2):
        j = 2 * pl.program_id(0) + t
        for half, weights in ((core[0], own), (1 - core[0], other)):
            here = weights[j // 2, :, t].reshape(KV, LANES)
            back = jnp.dot(dpre[...], here, preferred_element_type=F32)
            for k in range(LANES // 128):
                cols = slice(k * 128, (k + 1) * 128)
                into = pl.ds(pl.multiple_of((2 * t + half) * LANES + k * 128, 128), 128)
                less = normed[half, j, :, cols].astype(F32) * coef[...]
                grad[:, into] = ((back[:, cols] - less) * inv[...]).astype(BF16)


def grad_call(core, normed, dpre, inv, coef, own, other):
    return pl.pallas_call(
        grad_kernel,
        grid=(STEPS // 2,),
        in_specs=[SMEM] + [VMEM] * 6,
        out_specs=pl.BlockSpec((ROWS, 4 * LANES), lambda j: (0, j)),
        out_shape=jax.ShapeDtypeStruct((ROWS, D), BF16),
        compiler_params=params(16),
        cost_estimate=pl.CostEstimate(flops=2 * ROWS * D * KV, bytes_accessed=18 * MIB, transcendentals=0),
        name="input_gradient",
    )(core, *map(stay, (normed, dpre, inv, coef, own, other)))


def hop(value, first, second, distance):
    pairs = []
    for x in range(4):
        for y in range(4):
            for z in range(4):
                for core in range(2):
                    there = [x, y, z]
                    axis = first if core == 0 else second
                    there[axis] = (there[axis] + distance) % 4
                    pairs.append(tuple(flat(*at, core) for at in ((x, y, z), there)))
    return lax.ppermute(value, AXES, pairs)


def flat(x, y, z, core):
    return ((((x // 2) * 4 + y) * 2 + core) * 4 + z) * 2 + x % 2


def swap_cores(value):
    return lax.ppermute(value, "c", [(0, 1), (1, 0)])


X, Y, Z = 0, 1, 2


def shards(tokens, key_weight, cotangent):
    barrier = lax.optimization_barrier
    one = lambda value: value.astype(jnp.int32).reshape(1)
    index = lax.axis_index
    core, y, z, x = one(index("c")), one(index("y")), one(index("z")), one(index("xh") * 2 + index("xl"))
    first, odd, far = core[0] == 0, (x[0] & 1) == 1, (x[0] & 2) == 2
    cosine, sine = rope_tables((index("z") * 2 + index("xl")) * ROWS, ROWS)

    rows = key_weight.T
    left, right = rows[:, :LANES], rows[:, LANES:]
    came = swap_cores(jnp.where(first, right, left))
    pair = jnp.where(first, jnp.stack([left, came]), jnp.stack([came, right]))

    tokens, pair, core, y, z, x, first, odd, far, cosine, sine = barrier(
        (tokens, pair, core, y, z, x, first, odd, far, cosine, sine)
    )
    ring = [pair] + [hop(pair, X, X, -r) for r in (1, 2, 3)]
    normed, inv, dpre, dpre_t = prepare_call(tokens, cotangent, cosine, sine)
    for bit, step in ((odd, 1), (far, 2)):
        ring = [jnp.where(bit, ring[(i - step) % 4], ring[i]) for i in range(4)]
    near = jnp.stack(ring).reshape(2, 2, 2, 32, LANES)

    near, normed = barrier((near, normed))
    line = jnp.stack([near] + [hop(near, Y, Z, -r) for r in (1, 2, 3)])
    send = terms_call(core, normed, dpre_t, True)

    line, send = barrier((line, send))
    above, below = hop(line, Z, Y, -1), hop(line, Z, Y, 1)
    came = swap_cores(send)
    kept = terms_call(core, normed, dpre_t, False)
    own, up, down, far_up, far_down = add_call(core, x, y, kept, came)

    from_below, from_above = hop(far_up, X, Y, 1), hop(far_down, X, Y, -1)
    above, below = barrier((above, below, own))[:2]
    across = hop(above[:2], Z, Y, -1), hop(below[2:], Z, Y, 1)
    up, down = pass_on(up, down, from_below, from_above)
    arrived = [own, hop(up, X, Y, 1), hop(down, X, Y, -1)]
    weights = assemble(core, y, z, [line, above, below, across[0], across[1]])
    so_far = own_call(core, normed, weights)
    others = swap_cores(barrier((weights, so_far))[0])
    keys, coef = keys_call(core, normed, dpre, cosine, sine, others, so_far)
    cut = sum_cut(core, x, y, arrived)
    arrived = [cut[0]] + [hop(cut[r], Y, X, r) for r in (1, 3, 2)]
    arrived, coef = barrier((arrived, coef))
    cut = cut_call(z, arrived)
    arrived = [cut[0]] + [hop(cut[r], Z, Z, r) for r in (1, 3, 2)]
    grad = grad_call(core, normed, dpre, inv, coef, weights, others)
    arrived, grad = barrier((arrived, grad))
    total = sum(part.astype(F32) for part in arrived) * (1.0 / 256.0)
    mine = jnp.where(first, total[0], total[1])
    came = swap_cores(jnp.where(first, total[1], total[0]))
    summed = jnp.where(
        first, jnp.concatenate([mine, came], 1), jnp.concatenate([came, mine], 1)
    )
    return keys, grad, summed.T


def solution(mesh):
    fine = Mesh(mesh.devices.reshape(2, 4, 2, 4, 2), AXES)
    rows = P(AXES, None)
    weight = P(("z", "xl"), ("xh", "y", "c"))
    return jax.shard_map(
        shards,
        mesh=fine,
        in_specs=(rows, weight, rows),
        out_specs=(rows, rows, weight),
        check_vma=False,
    )
```

```python
import math

import jax
import jax.numpy as jnp
from jax import lax
from jax.experimental import pallas as pl
from jax.experimental.pallas import tpu as pltpu
from jax.sharding import Mesh
from jax.sharding import PartitionSpec as P

HEAD = 128
KV_HEADS = 4
SEQ = 4096
EPS = 1e-05
D = 8192
KV = 512
ROWS = 512
LANES = 512
STEPS = D // (2 * LANES)
AXES = ("xh", "y", "c", "z", "xl")
MIB = 1 << 20
F32 = jnp.float32
BF16 = jnp.bfloat16


def rope_tables(start, count):
    position = ((start + jnp.arange(count, dtype=jnp.int32)) % SEQ).astype(F32)
    half = HEAD // 2
    inv_freq = jnp.exp(-math.log(10000.0) * jnp.arange(half, dtype=F32) / half)
    angle = position[:, None] * inv_freq[None, :]
    return jnp.cos(angle), jnp.sin(angle)


def both_halves(cosine, sine):
    cos, sin = cosine[...], sine[...]
    return jnp.concatenate([cos, cos], 1), jnp.concatenate([-sin, sin], 1)


def rotate(values, cosine, sine):
    return values * cosine + pltpu.roll(values, HEAD // 2, 1) * sine


def params(mib):
    return pltpu.CompilerParams(vmem_limit_bytes=mib * MIB)


SMEM = pl.BlockSpec(memory_space=pltpu.SMEM)


VMEM = pl.BlockSpec(memory_space=pltpu.VMEM)


def stay(value):
    return pltpu.with_memory_space_constraint(value, pltpu.VMEM)


def prepare_kernel(x, cot, cosine, sine, normed, inv, dpre, dpre_t):
    rows = pl.ds(pl.multiple_of(pl.program_id(0) * 128, 128), 128)
    acc = jnp.zeros((128, 128), F32)
    for k in range(D // 128):
        wide = x[:, k * 128 : (k + 1) * 128].astype(F32)
        acc += wide * wide
    scale = lax.rsqrt(jnp.sum(acc, axis=1, keepdims=True) / D + EPS)
    scale = jnp.broadcast_to(scale, (128, 128))
    inv[rows, :] = scale
    for k in range(D // 128):
        part, col = divmod(k * 128, LANES)
        value = x[:, k * 128 : (k + 1) * 128].astype(F32) * scale
        normed[part % 2, part // 2, rows, col : col + 128] = value.astype(BF16)
    cos, sin = both_halves(cosine, sine)
    for head in range(KV_HEADS):
        cols = slice(head * HEAD, (head + 1) * HEAD)
        turned = rotate(cot[:, cols].astype(F32), cos, -sin)
        dpre[rows, cols] = turned.astype(BF16)
        dpre_t[cols, rows] = turned.T.astype(BF16)


def prepare_call(tokens, cot, cosine, sine):
    rows = lambda width: pl.BlockSpec((128, width), lambda j: (j, 0))
    return pl.pallas_call(
        prepare_kernel,
        grid=(ROWS // 128,),
        in_specs=[rows(D), rows(KV), rows(HEAD // 2), rows(HEAD // 2)],
        out_specs=[VMEM] * 4,
        out_shape=[
            pltpu.VMEM((2, STEPS, ROWS, LANES), BF16),
            pltpu.VMEM((ROWS, 128), F32),
            pltpu.VMEM((ROWS, KV), BF16),
            pltpu.VMEM((KV, ROWS), BF16),
        ],
        compiler_params=params(16),
        cost_estimate=pl.CostEstimate(flops=10 * ROWS * D, bytes_accessed=18 * MIB, transcendentals=0),
        name="row_scales",
    )(
        pltpu.with_memory_space_constraint(tokens, pltpu.HBM),
        pltpu.with_memory_space_constraint(cot, pltpu.HBM),
        cosine,
        sine,
    )


def terms_call(core, normed, dpre_t, other):
    def kernel(core, normed, dpre_t, out):
        half = 1 - core[0] if other else core[0]

        @pl.loop(0, STEPS)
        def _(i):
            term = jnp.dot(dpre_t[...], normed[half, i], preferred_element_type=F32)
            out[i] = term.astype(BF16).reshape(16, 32, LANES)

    return pl.pallas_call(
        kernel,
        in_specs=[SMEM, VMEM, VMEM],
        out_specs=VMEM,
        out_shape=pltpu.VMEM((STEPS, 16, 32, LANES), BF16),
        compiler_params=params(8),
        cost_estimate=pl.CostEstimate(flops=ROWS * D * KV, bytes_accessed=9 * MIB, transcendentals=0),
        name="send_half" if other else "keep_half",
    )(core, stay(normed), stay(dpre_t))


def add_kernel(core, x, y, kept, came, own, up, down, far_up, far_down):
    first = core[0] == 0

    @pl.loop(0, 16)
    def _(n):
        a, b = n // 4, n % 4
        for r in range(4):
            x_at = jnp.where(first, (x[0] + r) % 4, a)
            y_at = jnp.where(first, a, (y[0] + r) % 4)
            at = (2 * b + x_at % 2, pl.ds(8 * (x_at // 2) + 2 * y_at, 2))
            block = kept[at] + came[at]
            if r != 2:
                {0: own, 1: up, 3: down}[r][a, b] = block
                continue

            @pl.when(a < 2)
            def _():
                far_up[a, b] = block

            @pl.when(a >= 2)
            def _():
                far_down[a - 2, b] = block


def add_call(core, x, y, kept, came):
    part, half = (4, 4, 2, 32, LANES), (2, 4, 2, 32, LANES)
    return pl.pallas_call(
        add_kernel,
        in_specs=[SMEM] * 3 + [VMEM] * 2,
        out_specs=[VMEM] * 5,
        out_shape=[pltpu.VMEM(part, BF16)] * 3 + [pltpu.VMEM(half, BF16)] * 2,
        compiler_params=params(16),
        cost_estimate=pl.CostEstimate(flops=0, bytes_accessed=12 * MIB, transcendentals=0),
        name="add_cores",
    )(core, x, y, stay(kept), stay(came))


def pass_on_kernel(up, down, from_below, from_above, up_out, down_out):
    up_out[:2] = (up[:2].astype(F32) + from_below[...].astype(F32)).astype(BF16)
    down_out[2:] = (down[2:].astype(F32) + from_above[...].astype(F32)).astype(BF16)


def pass_on(up, down, from_below, from_above):
    return pl.pallas_call(
        pass_on_kernel,
        in_specs=[VMEM] * 4,
        out_specs=[VMEM] * 2,
        out_shape=[pltpu.VMEM(up.shape, BF16)] * 2,
        input_output_aliases={0: 0, 1: 1},
        compiler_params=params(8),
        cost_estimate=pl.CostEstimate(flops=0, bytes_accessed=3 * MIB, transcendentals=0),
        name="pass_on",
    )(*map(stay, (up, down, from_below, from_above)))


def sum_cut_kernel(core, x, y, own, one, two, *outs):
    base = jnp.where(core[0] == 0, y[0], x[0])
    for r in range(4):
        k = (base + r) % 4
        total = own[k].astype(F32) + one[k].astype(F32) + two[k].astype(F32)
        outs[r][...] = total.astype(BF16)


def sum_cut(core, x, y, parts):
    shape = parts[0].shape
    return pl.pallas_call(
        sum_cut_kernel,
        in_specs=[SMEM] * 3 + [VMEM] * 3,
        out_specs=[VMEM] * 4,
        out_shape=[pltpu.VMEM(shape[1:], BF16)] * 4,
        compiler_params=params(8),
        cost_estimate=pl.CostEstimate(flops=64424509440, bytes_accessed=125829120, transcendentals=0),
        name="sum_first",
    )(core, x, y, *map(stay, parts))


def cut_kernel(z, one, two, three, four, *outs):
    for r in range(4):
        k = (z[0] + r) % 4
        total = one[k].astype(F32) + two[k].astype(F32)
        outs[r][...] = (total + three[k].astype(F32) + four[k].astype(F32)).astype(BF16)


def cut_call(z, parts):
    shape = parts[0].shape
    return pl.pallas_call(
        cut_kernel,
        in_specs=[SMEM] + [VMEM] * 4,
        out_specs=[VMEM] * 4,
        out_shape=[pltpu.VMEM(shape[1:], BF16)] * 4,
        compiler_params=params(8),
        cost_estimate=pl.CostEstimate(flops=0, bytes_accessed=2 * MIB, transcendentals=0),
        name="sum_second",
    )(z, *map(stay, parts))


def assemble_kernel(core, y, z, *refs):
    pieces, out = refs[:5], refs[5]
    for piece, r, start in zip(pieces, (0, 1, 3, 2, 2), (0, 0, 0, 0, 2)):

        @pl.loop(0, piece.shape[0])
        def _(i):
            k = i + start
            down, along = jnp.where(core[0] == 0, r, k), jnp.where(core[0] == 0, k, r)
            out[(z[0] + down) % 4, :, :, (y[0] + along) % 4] = piece[i]


def assemble(core, y, z, pieces):
    return pl.pallas_call(
        assemble_kernel,
        in_specs=[SMEM] * 3 + [VMEM] * 5,
        out_specs=VMEM,
        out_shape=pltpu.VMEM((4, 2, 2, 4, 2, 32, LANES), BF16),
        compiler_params=params(8),
        cost_estimate=pl.CostEstimate(flops=0, bytes_accessed=8 * MIB, transcendentals=0),
        name="assemble",
    )(core, y, z, *map(stay, pieces))


def products(half, normed, weights, pre):
    @pl.loop(0, 4)
    def _(n):
        part = None
        for xl in range(2):
            term = lax.dot_general(
                normed[half, 2 * n + xl],
                weights[n, :, xl].reshape(KV, LANES),
                (((1,), (1,)), ((), ())),
                preferred_element_type=F32,
            )
            part = term if part is None else part + term
        pre[...] += part


def own_kernel(core, normed, weights, pre):
    pre[...] = jnp.zeros_like(pre)
    products(core[0], normed, weights, pre)


def own_call(core, normed, weights):
    return pl.pallas_call(
        own_kernel,
        in_specs=[SMEM] + [VMEM] * 2,
        out_specs=VMEM,
        out_shape=pltpu.VMEM((ROWS, KV), F32),
        compiler_params=params(12),
        cost_estimate=pl.CostEstimate(flops=6442450944, bytes_accessed=12582912, transcendentals=0),
        name="keys_own_half",
    )(core, stay(normed), stay(weights))


def keys_kernel(core, normed, dpre, cosine, sine, weights, so_far, keys, coef, pre):
    pre[...] = so_far[...]
    products(1 - core[0], normed, weights, pre)
    total = jnp.zeros((ROWS, HEAD), F32)
    cos, sin = both_halves(cosine, sine)
    for head in range(KV_HEADS):
        cols = slice(head * HEAD, (head + 1) * HEAD)
        values = pre[:, cols]
        keys[:, cols] = rotate(values, cos, sin).astype(BF16)
        total += values * dpre[:, cols].astype(F32)
    coef[...] = jnp.broadcast_to(jnp.sum(total, axis=1, keepdims=True) / D, (ROWS, 128))


def keys_call(core, normed, dpre, cosine, sine, weights, so_far):
    return pl.pallas_call(
        keys_kernel,
        in_specs=[SMEM] + [VMEM] * 6,
        out_specs=[VMEM] * 2,
        out_shape=[
            jax.ShapeDtypeStruct((ROWS, KV), BF16),
            pltpu.VMEM((ROWS, 128), F32),
        ],
        scratch_shapes=[pltpu.VMEM((ROWS, KV), F32)],
        compiler_params=params(12),
        cost_estimate=pl.CostEstimate(flops=ROWS * D * KV, bytes_accessed=9 * MIB, transcendentals=0),
        name="keys",
    )(core, stay(normed), stay(dpre), cosine, sine, stay(weights), stay(so_far))


def grad_kernel(core, normed, dpre, inv, coef, own, other, grad):
    for t in range(2):
        j = 2 * pl.program_id(0) + t
        for half, weights in ((core[0], own), (1 - core[0], other)):
            here = weights[j // 2, :, t].reshape(KV, LANES)
            back = jnp.dot(dpre[...], here, preferred_element_type=F32)
            for k in range(LANES // 128):
                cols = slice(k * 128, (k + 1) * 128)
                into = pl.ds(pl.multiple_of((2 * t + half) * LANES + k * 128, 128), 128)
                less = normed[half, j, :, cols].astype(F32) * coef[...]
                grad[:, into] = ((back[:, cols] - less) * inv[...]).astype(BF16)


def grad_call(core, normed, dpre, inv, coef, own, other):
    return pl.pallas_call(
        grad_kernel,
        grid=(STEPS // 2,),
        in_specs=[SMEM] + [VMEM] * 6,
        out_specs=pl.BlockSpec((ROWS, 4 * LANES), lambda j: (0, j)),
        out_shape=jax.ShapeDtypeStruct((ROWS, D), BF16),
        compiler_params=params(16),
        cost_estimate=pl.CostEstimate(flops=2 * ROWS * D * KV, bytes_accessed=18 * MIB, transcendentals=0),
        name="input_gradient",
    )(core, *map(stay, (normed, dpre, inv, coef, own, other)))


def hop(value, first, second, distance):
    pairs = []
    for x in range(4):
        for y in range(4):
            for z in range(4):
                for core in range(2):
                    there = [x, y, z]
                    axis = first if core == 0 else second
                    there[axis] = (there[axis] + distance) % 4
                    pairs.append(tuple(flat(*at, core) for at in ((x, y, z), there)))
    return lax.ppermute(value, AXES, pairs)


def flat(x, y, z, core):
    return ((((x // 2) * 4 + y) * 2 + core) * 4 + z) * 2 + x % 2


def swap_cores(value):
    return lax.ppermute(value, "c", [(0, 1), (1, 0)])


X, Y, Z = 0, 1, 2


def shards(tokens, key_weight, cotangent):
    barrier = lax.optimization_barrier
    one = lambda value: value.astype(jnp.int32).reshape(1)
    index = lax.axis_index
    core, y, z, x = one(index("c")), one(index("y")), one(index("z")), one(index("xh") * 2 + index("xl"))
    first, odd, far = core[0] == 0, (x[0] & 1) == 1, (x[0] & 2) == 2
    cosine, sine = rope_tables((index("z") * 2 + index("xl")) * ROWS, ROWS)

    rows = key_weight.T
    left, right = rows[:, :LANES], rows[:, LANES:]
    came = swap_cores(jnp.where(first, right, left))
    pair = jnp.where(first, jnp.stack([left, came]), jnp.stack([came, right]))

    tokens, pair, core, y, z, x, first, odd, far, cosine, sine = barrier(
        (tokens, pair, core, y, z, x, first, odd, far, cosine, sine)
    )
    ring = [pair] + [hop(pair, X, X, -r) for r in (1, 2, 3)]
    normed, inv, dpre, dpre_t = prepare_call(tokens, cotangent, cosine, sine)
    for bit, step in ((odd, 1), (far, 2)):
        ring = [jnp.where(bit, ring[(i - step) % 4], ring[i]) for i in range(4)]
    near = jnp.stack(ring).reshape(2, 2, 2, 32, LANES)

    near, normed = barrier((near, normed))
    hops = {r: hop(near, Y, Z, -r) for r in (1, 3, 2)}
    line = jnp.stack([near] + [hops[r] for r in (1, 2, 3)])
    send = terms_call(core, normed, dpre_t, True)

    line, send = barrier((line, send))
    above, below = hop(line, Z, Y, -1), hop(line, Z, Y, 1)
    came = swap_cores(send)
    kept = terms_call(core, normed, dpre_t, False)
    own, up, down, far_up, far_down = add_call(core, x, y, kept, came)

    from_below, from_above = hop(far_up, X, Y, 1), hop(far_down, X, Y, -1)
    above, below = barrier((above, below, own))[:2]
    across = hop(above[:2], Z, Y, -1), hop(below[2:], Z, Y, 1)
    up, down = pass_on(up, down, from_below, from_above)
    arrived = [own, hop(up, X, Y, 1), hop(down, X, Y, -1)]
    weights = assemble(core, y, z, [line, above, below, across[0], across[1]])
    so_far = own_call(core, normed, weights)
    others = swap_cores(barrier((weights, so_far))[0])
    keys, coef = keys_call(core, normed, dpre, cosine, sine, others, so_far)
    cut = sum_cut(core, x, y, arrived)
    arrived = [cut[0]] + [hop(cut[r], Y, X, r) for r in (1, 3, 2)]
    arrived, coef = barrier((arrived, coef))
    cut = cut_call(z, arrived)
    arrived = [cut[0]] + [hop(cut[r], Z, Z, r) for r in (1, 3, 2)]
    grad = grad_call(core, normed, dpre, inv, coef, weights, others)
    arrived, grad = barrier((arrived, grad))
    total = sum(part.astype(F32) for part in arrived) * (1.0 / 256.0)
    mine = jnp.where(first, total[0], total[1])
    came = swap_cores(jnp.where(first, total[1], total[0]))
    summed = jnp.where(
        first, jnp.concatenate([mine, came], 1), jnp.concatenate([came, mine], 1)
    )
    return keys, grad, summed.T


def solution(mesh):
    fine = Mesh(mesh.devices.reshape(2, 4, 2, 4, 2), AXES)
    rows = P(AXES, None)
    weight = P(("z", "xl"), ("xh", "y", "c"))
    return jax.shard_map(
        shards,
        mesh=fine,
        in_specs=(rows, weight, rows),
        out_specs=(rows, rows, weight),
        check_vma=False,
    )
```
